32 devices in a mesh: groups: 1, vocab: 32 (over z, y, x, core).
Axes of the slice: x: 2, y: 2, z: 4, core: 2. Of those that a mesh axis runs over, the one named last changes fastest.
Arguments:
- policy_hidden: bfloat16 [512, 5120], P(('groups', 'vocab')), may hold values from -62 to 62
- frozen_hidden: bfloat16 [512, 5120], P(('groups', 'vocab')), may hold values from -62 to 62
- policy_head: bfloat16 [20480, 5120], P('vocab'), may hold values from -2.51557647 to 2.51557647
- frozen_head: bfloat16 [20480, 5120], P('vocab'), may hold values from -2.51557647 to 2.51557647
- actions: int32 [512], P('groups'), may hold values from 0 to 20479
- behavior_logprob: float32 [512], P('groups'), may hold values from -19 to -13
- advantage_sign: int32 [512], P('groups'), may hold values from 0 to 1
- advantage_size: float32 [512], P('groups'), may hold values from 0.2 to 2
- response_mask: int32 [512], P('groups'), may hold values 0 or 1
Outputs:
- hidden_grad: bfloat16 [512, 5120], P(('groups', 'vocab'))
- surrogate_loss: float32 [1], P('groups')
The draws below stay inside these ranges and needn't reach their ends.
All inputs are finite; a program needn't handle non-finite values.
Results may differ from the reference program's by a relative error of at most 0.0053.
Values may be sent and summed in bfloat16 or wider, within the bound.
A program may use at most 128 MiB of HBM per device.

```python
import math
import jax
import jax.numpy as jnp

D = 5120
TOKENS = 512
VOCAB = 20480


def sign_pattern(width):
    return 1.0 - 2.0 * (jnp.arange(width) % 2).astype(jnp.float32)


def hidden_rows(key, spread):
    first, second = jax.random.split(key, 2)
    base = jnp.clip(jax.random.normal(first, (TOKENS, D), jnp.float32), -6.0, 6.0)
    scales = jnp.exp(jax.random.uniform(second, (TOKENS, 1), jnp.float32) * jnp.log(spread))
    return (base * scales).astype(jnp.bfloat16)


def head_rows(key, spread, strength, higher, lower):
    first, second = jax.random.split(key, 2)
    base = jnp.clip(jax.random.normal(first, (VOCAB, D), jnp.float32), -6.0, 6.0) * (3.0 / D ** 0.5)
    scales = jnp.exp(jax.random.uniform(second, (VOCAB, 1), jnp.float32) * jnp.log(spread))
    where_row = jnp.arange(VOCAB) % 512
    aligned = ((where_row == 5) | (where_row == 6)).astype(jnp.float32)[:, None]
    height = jnp.where(where_row == 5, higher, jnp.where(where_row == 6, lower, 0.0))[:, None]
    keep = 1.0 - strength * aligned
    return (base * scales * keep + strength * height * sign_pattern(D)[None, :] / D).astype(jnp.bfloat16)


def draw_policy_hidden(key, part):
    key = jax.random.fold_in(key, 11)
    return hidden_rows(key, 1.0)


def draw_frozen_hidden(key, part):
    key = jax.random.fold_in(key, 12)
    return hidden_rows(key, 1.0)


def draw_policy_head(key, part):
    key = jax.random.fold_in(key, 21)
    return head_rows(key, 1.0, 0.0, 0.0, 0.0)


def draw_frozen_head(key, part):
    key = jax.random.fold_in(key, 22)
    return head_rows(key, 1.0, 0.0, 0.0, 0.0)


def touch_ends(result, key, smallest, high):
    dims = result.shape
    spot = [jax.random.randint(jax.random.fold_in(key, axis), (), 0, dims[axis]) for axis in range(len(dims))]
    result = result.at[tuple(spot)].set(smallest)
    longest = dims.index(max(dims))
    spot[longest] = (spot[longest] + 1) % dims[longest]
    return result.at[tuple(spot)].set(high)


def setup_inputs(seed: int = 0, part: int = 0) -> dict:
    splits = jax.random.split(jax.random.key(seed), 10)
    own_keys = jax.random.split(jax.random.fold_in(splits[9], part), 10)
    policy_hidden = draw_policy_hidden(jax.random.fold_in(jax.random.fold_in(splits[9], part), 71), part)
    frozen_hidden = draw_frozen_hidden(jax.random.fold_in(jax.random.fold_in(splits[9], part), 71), part)
    policy_head = draw_policy_head(jax.random.fold_in(splits[9], 71), part)
    frozen_head = draw_frozen_head(jax.random.fold_in(splits[9], 71), part)
    actions = touch_ends(jax.random.randint(own_keys[4], (TOKENS,), 0, VOCAB), jax.random.fold_in(own_keys[4], 1), 0, VOCAB - 1).astype(jnp.int32)
    behavior_logprob = jnp.clip(jax.random.uniform(own_keys[5], (TOKENS,), jnp.float32, -19.0, -13.0), -19.0, -13.0)
    advantage_sign = touch_ends(jax.random.randint(own_keys[6], (TOKENS,), 0, 2), jax.random.fold_in(own_keys[6], 1), 0, 1).astype(jnp.int32)
    advantage_size = jnp.clip(jnp.exp(jax.random.uniform(own_keys[7], (TOKENS,), jnp.float32, math.log(0.2), math.log(2.0))), 0.2, 2.0)
    response_mask = touch_ends((jax.random.randint(own_keys[8], (TOKENS,), 0, 4) < 3).astype(jnp.int32), jax.random.fold_in(own_keys[8], 1), 0, 1)
    return dict(policy_hidden=policy_hidden, frozen_hidden=frozen_hidden, policy_head=policy_head, frozen_head=frozen_head, actions=actions, behavior_logprob=behavior_logprob, advantage_sign=advantage_sign, advantage_size=advantage_size, response_mask=response_mask)


clip_eps = 0.2
dual_bound = 3.0
kl_weight = 0.1
loss_scale = 16.0


def surrogate(picked_logp, behavior_logprob, advantage_sign, advantage_size):
    advantage = (2 * advantage_sign - 1).astype(jnp.float32) * advantage_size
    ratio = jnp.exp(picked_logp - behavior_logprob)
    clipped = jnp.clip(ratio, 1.0 - clip_eps, 1.0 + clip_eps)
    primary = jnp.maximum(-advantage * ratio, -advantage * clipped)
    objective = jnp.where(advantage < 0, jnp.minimum(primary, -dual_bound * advantage), primary)
    upward = (advantage > 0) & (ratio <= 1.0 + clip_eps)
    downward = (advantage < 0) & (ratio >= 1.0 - clip_eps) & (ratio <= dual_bound)
    slope = jnp.where(upward | downward, -advantage * ratio, jnp.zeros_like(ratio))
    return objective, slope


def log_total(logits):
    peak = jnp.max(logits, axis=1, keepdims=True)
    return peak[:, 0] + jnp.log(jnp.sum(jnp.exp(logits - peak), axis=1))


def reference(policy_hidden, frozen_hidden, policy_head, frozen_head, actions, behavior_logprob, advantage_sign, advantage_size, response_mask):
    policy_logits = jnp.dot(policy_hidden, policy_head.T, preferred_element_type=jnp.float32)
    frozen_logits = jnp.dot(frozen_hidden, frozen_head.T, preferred_element_type=jnp.float32)
    policy_lse = log_total(policy_logits)
    frozen_lse = log_total(frozen_logits)
    policy_prob = jnp.exp(policy_logits - policy_lse[:, None])
    log_gap = policy_logits - frozen_logits - policy_lse[:, None] + frozen_lse[:, None]
    divergence = jnp.sum(policy_prob * log_gap, axis=1)
    columns = jnp.arange(VOCAB, dtype=jnp.int32)
    chosen = actions[:, None] == columns[None, :]
    picked = jnp.sum(jnp.where(chosen, policy_logits, jnp.zeros_like(policy_logits)), axis=1)
    objective, slope = surrogate(picked - policy_lse, behavior_logprob, advantage_sign, advantage_size)
    weight = response_mask.astype(jnp.float32)
    surrogate_loss = jnp.sum(weight * (objective + kl_weight * divergence)).reshape(1)
    logit_grad = (loss_scale * weight)[:, None] * (slope[:, None] * (chosen.astype(jnp.float32) - policy_prob) + kl_weight * policy_prob * (log_gap - divergence[:, None]))
    logit_grad = logit_grad.astype(jnp.bfloat16)
    hidden_grad = jnp.dot(logit_grad, policy_head, preferred_element_type=jnp.float32).astype(jnp.bfloat16)
    return hidden_grad, surrogate_loss
```

```python
import jax
import jax.numpy as jnp
from jax import lax
from jax.experimental import pallas as pl
from jax.experimental.pallas import tpu as pltpu
from jax.sharding import PartitionSpec as P

clip_eps = 0.2
dual_bound = 3.0
kl_weight = 0.1
loss_scale = 16.0


def head_product(rows_block, head):
    return lax.dot_general(
        rows_block, head, (((1,), (1,)), ((), ())), preferred_element_type=jnp.float32
    )


def surrogate(picked_logp, behavior_logprob, advantage_sign, advantage_size):
    advantage = (2 * advantage_sign - 1).astype(jnp.float32) * advantage_size
    ratio = jnp.exp(picked_logp - behavior_logprob)
    clipped = jnp.clip(ratio, 1.0 - clip_eps, 1.0 + clip_eps)
    primary = jnp.maximum(-advantage * ratio, -advantage * clipped)
    objective = jnp.where(advantage < 0, jnp.minimum(primary, -dual_bound * advantage), primary)
    upward = (advantage > 0) & (ratio <= 1.0 + clip_eps)
    downward = (advantage < 0) & (ratio >= 1.0 - clip_eps) & (ratio <= dual_bound)
    slope = jnp.where(upward | downward, -advantage * ratio, jnp.zeros_like(ratio))
    return (objective, slope)


def local_sums(policy_logits, frozen_logits, policy_peak, frozen_peak, chosen):
    policy_exp = jnp.exp(policy_logits - policy_peak[:, None])
    policy_total = jnp.sum(policy_exp, axis=1)
    gap_total = jnp.sum(policy_exp * (policy_logits - frozen_logits), axis=1)
    frozen_total = jnp.sum(jnp.exp(frozen_logits - frozen_peak[:, None]), axis=1)
    picked = jnp.sum(jnp.where(chosen, policy_logits, jnp.zeros_like(policy_logits)), axis=1)
    return (policy_total, gap_total, frozen_total, picked)


def shards(
    policy_hidden,
    frozen_hidden,
    policy_head,
    frozen_head,
    actions,
    behavior_logprob,
    advantage_sign,
    advantage_size,
    response_mask,
):
    own_rows = policy_hidden.shape[0]
    vocab_rows = policy_head.shape[0]
    policy_all, frozen_all = (
        lax.all_gather(policy_hidden, "vocab", axis=0, tiled=True),
        lax.all_gather(frozen_hidden, "vocab", axis=0, tiled=True),
    )
    policy_logits = head_product(policy_all, policy_head)
    frozen_logits = head_product(frozen_all, frozen_head)
    offset = lax.axis_index("vocab") * vocab_rows
    columns = offset + jnp.arange(vocab_rows, dtype=jnp.int32)
    chosen = actions[:, None] == columns[None, :]
    policy_local = jnp.max(policy_logits, axis=1)
    frozen_local = jnp.max(frozen_logits, axis=1)
    policy_peak, frozen_peak = lax.pmax((policy_local, frozen_local), "vocab")
    sums_here = local_sums(policy_logits, frozen_logits, policy_peak, frozen_peak, chosen)
    policy_total, gap_total, frozen_total, picked = lax.psum(
        (sums_here[0], sums_here[1], sums_here[2], sums_here[3]), "vocab"
    )
    policy_lse = policy_peak + jnp.log(policy_total)
    frozen_lse = frozen_peak + jnp.log(frozen_total)
    divergence = gap_total / policy_total - policy_lse + frozen_lse
    objective, slope = surrogate(
        picked - policy_lse, behavior_logprob, advantage_sign, advantage_size
    )
    weight = response_mask.astype(jnp.float32)
    surrogate_loss = jnp.sum(weight * (objective + kl_weight * divergence)).reshape(1)
    policy_prob = jnp.exp(policy_logits - policy_lse[:, None])
    log_gap = policy_logits - frozen_logits - policy_lse[:, None] + frozen_lse[:, None]
    logit_grad = (loss_scale * weight)[:, None] * (
        slope[:, None] * (chosen.astype(jnp.float32) - policy_prob)
        + kl_weight * policy_prob * (log_gap - divergence[:, None])
    )
    logit_grad = logit_grad.astype(jnp.bfloat16)
    partial_grad = jnp.dot(logit_grad, policy_head, preferred_element_type=jnp.float32)
    summed = lax.psum(partial_grad, "vocab")
    hidden_grad = lax.dynamic_slice_in_dim(summed, lax.axis_index("vocab") * own_rows, own_rows, 0)
    return (hidden_grad.astype(jnp.bfloat16), surrogate_loss)


MESH = pl.DeviceIdType.MESH
f32 = jnp.float32
bf16 = jnp.bfloat16
GATHER = ((0, 0, "zxy"), (0, 1, "zyx"), (1, 0, "xzy"), (1, 1, "yzx"))
SCATTER = ("yxz", "xyz", "yzx", "xzy")


def nt_dot(a, b):
    return lax.dot_general(a, b, (((1,), (1,)), ((), ())), preferred_element_type=f32)


def gather_events():
    events = []
    for part, (_, _, order) in enumerate(GATHER):
        for dz in range(-3, 4):
            for dy in range(2):
                for dx in range(2):
                    moved = {"z": dz, "y": dy, "x": dx}
                    last = max([order.index(a) for a in order if moved[a]], default=-1)
                    onward = order[last + 1 :]
                    depth = abs(dz) + dy + dx
                    events.append((depth, part, dz, dy, dx, order[last] if last >= 0 else "", onward))
    events.sort(key=lambda e: (e[0], e[1]))
    return events


def kernel(
    ph, fh, pw_hbm, fw_hbm, act, beh, sgn, siz, msk,
    out, loss,
    hid, pw, fw, pl_acc, fl_acc, cols, rows, grad, st1, st2,
    sib_out, sib_in, acc, s1, r1, s2, r2, zs, zr,
    load_sem, g_send, g_recv, g_sib, st_send, st_recv, st2_send, st2_recv,
    sib_send, sib_recv, s1_send, s1_recv, s2_send, s2_recv, z_send, z_recv,
):
    tokens, vocab_rows = pl_acc.shape
    width = ph.shape[1]
    half, quarter = width // 2, width // 4
    me = lax.axis_index("vocab")
    c, x, y, z = me % 2, (me // 2) % 2, (me // 4) % 2, me // 8
    plane = me % 8

    def dev(zz, yy, xx, cc):
        return {"vocab": ((zz * 2 + yy) * 2 + xx) * 2 + cc}

    sibling = dev(z, y, x, 1 - c)

    def put(src, dst, send, recv, where):
        return pltpu.make_async_remote_copy(
            src_ref=src, dst_ref=dst, send_sem=send, recv_sem=recv,
            device_id=where, device_id_type=MESH,
        )

    load_p = pltpu.make_async_copy(pw_hbm, pw, load_sem.at[0])
    load_f = pltpu.make_async_copy(fw_hbm, fw, load_sem.at[1])
    load_p.start()
    load_f.start()
    barrier = pltpu.get_barrier_semaphore()
    for k in range(1, 8):
        pl.semaphore_signal(
            barrier, inc=1, device_id={"vocab": z * 8 + (plane + k) % 8}, device_id_type=MESH
        )
    for k in range(1, 4):
        pl.semaphore_signal(
            barrier, inc=1, device_id={"vocab": ((z + k) % 4) * 8 + plane}, device_id_type=MESH
        )
    hid[0, z, y, x, c] = ph[...]
    hid[1, z, y, x, c] = fh[...]
    pl.semaphore_wait(barrier, 10)

    def chunk(part, sz, sy, sx, sc):
        model, side, _ = GATHER[part]
        return hid.at[model, sz, sy, sx, sc, :, pl.ds(side * half, half)]

    def gather_copy(part, sz, sy, sx, way):
        where, slot = {
            "+": (dev(z + 1, y, x, c), 0),
            "-": (dev(z - 1, y, x, c), 1),
            "y": (dev(z, 1 - y, x, c), 2),
            "x": (dev(z, y, 1 - x, c), 3),
            "s": (sibling, 4),
        }[way]
        source = (sz * 2 + sy) * 2 + sx
        block = chunk(part, sz, sy, sx, c)
        if way == "s":
            _, _, order = GATHER[part]
            recv = g_sib.at[part, source]
        else:
            recv = g_recv.at[part, source]
        return put(block, block, g_send.at[part, source, slot], recv, where)

    def gather_event(event, act_on):
        _, part, dz, dy, dx, last, onward = event
        sz, sy, sx = z + dz, (1 - y if dy else y), (1 - x if dx else x)

        def go():
            if act_on == "start" and last:
                gather_copy(part, sz, sy, sx, "y").wait_recv()

            def each(way, cond=None):
                def run():
                    copy = gather_copy(part, sz, sy, sx, way)
                    if act_on == "start":
                        copy.start()
                    else:
                        copy.wait_send()

                if cond is None:
                    run()
                else:
                    pl.when(cond)(run)

            if ("z" in onward and dz == 0) or (last == "z" and dz < 0):
                each("+", z < 3)
            if ("z" in onward and dz == 0) or (last == "z" and dz > 0):
                each("-", z > 0)
            for way in onward:
                if way != "z":
                    each(way)
            each("s")

        if dz == 0:
            go()
        else:
            pl.when((sz >= 0) & (sz <= 3))(go)

    events = gather_events()
    for event in events:
        gather_event(event, "start")
        if event[0] == 0 and event[1] == 3:
            rows[...] = jnp.zeros_like(rows)
            rows[0:1, :] = act[...].astype(f32)
            for b in range(tokens // 128):
                span = pl.ds(b * 128, 128)
                cols[span, :] = rows[:, span].T

    def wait_sibling(part):
        @pl.loop(0, 16)
        def _(i):
            block = chunk(part, i // 4, (i // 2) % 2, i % 2, 1 - c)
            put(block, block, g_send.at[part, 0, 4], g_sib.at[part, i], sibling).wait_recv()

    load_p.wait()
    load_f.wait()
    tile = half // 2
    for part, (model, side, _) in enumerate(GATHER):
        wait_sibling(part)
        head, total = (pw, pl_acc) if model == 0 else (fw, fl_acc)

        @pl.loop(0, 2)
        def _(i):
            span = pl.ds(pl.multiple_of(side * half + i * tile, tile), tile)
            new = nt_dot(hid[model, :, :, :, :, :, span].reshape(tokens, tile), head[:, span])
            if side == 0:
                @pl.when(i == 0)
                def _():
                    total[...] = new

                @pl.when(i > 0)
                def _():
                    total[...] += new
            else:
                total[...] += new

    block_rows = 128
    first = (me * vocab_rows).astype(f32)

    def chosen_of(span):
        ids = lax.broadcasted_iota(jnp.int32, (block_rows, vocab_rows), 1).astype(f32) + first
        return cols[span, 0:1] == ids

    for b in range(tokens // block_rows):
        span = pl.ds(b * block_rows, block_rows)
        pol, fro = pl_acc[span, :], fl_acc[span, :]
        ppk = jnp.max(pol, axis=1, keepdims=True)
        fpk = jnp.max(fro, axis=1, keepdims=True)
        ex = jnp.exp(pol - ppk)
        stats = (
            ppk,
            jnp.sum(ex, axis=1, keepdims=True),
            jnp.sum(ex * (pol - fro), axis=1, keepdims=True),
            fpk,
            jnp.sum(jnp.exp(fro - fpk), axis=1, keepdims=True),
            jnp.sum(jnp.where(chosen_of(span), pol, 0.0), axis=1, keepdims=True),
        )
        lane = lax.broadcasted_iota(jnp.int32, (block_rows, 128), 1)
        packed = jnp.zeros((block_rows, 128), f32)
        for i, s in enumerate(stats):
            packed = jnp.where(lane == i, s, packed)
        st1[plane, :, b * block_rows : (b + 1) * block_rows] = packed.T[0:8, :]

    def combine(blocks):
        ppk, fpk = blocks[0][0:1], blocks[0][3:4]
        for blk in blocks[1:]:
            ppk, fpk = jnp.maximum(ppk, blk[0:1]), jnp.maximum(fpk, blk[3:4])
        pt = gap = ft = pick = 0.0
        for blk in blocks:
            scale = jnp.exp(blk[0:1] - ppk)
            pt = pt + scale * blk[1:2]
            gap = gap + scale * blk[2:3]
            ft = ft + jnp.exp(blk[3:4] - fpk) * blk[4:5]
            pick = pick + blk[5:6]
        return ppk, pt, gap, fpk, ft, pick

    def st1_copy(k, slot):
        where = {"vocab": z * 8 + (plane + k) % 8}
        return put(st1.at[slot], st1.at[slot], st_send.at[k], st_recv.at[slot], where)

    def st2_copy(k, slot):
        where = {"vocab": ((z + k) % 4) * 8 + plane}
        return put(st2.at[slot], st2.at[slot], st2_send.at[k], st2_recv.at[slot], where)

    for k in range(1, 8):
        st1_copy(k, plane).start()
    for event in events:
        gather_event(event, "finish")
    for k in range(1, 8):
        st1_copy(k, (plane + k) % 8).wait_recv()
    both = combine([st1[i] for i in range(8)])
    for i, s in enumerate(both):
        st2[z, i : i + 1, :] = s
    st2[z, 6:8, :] = jnp.zeros((2, tokens), f32)
    for k in range(1, 4):
        st2_copy(k, z).start()
    for k in range(1, 4):
        st2_copy(k, (z + k) % 4).wait_recv()
    ppk, pt, gap, fpk, ft, picked = combine([st2[i] for i in range(4)])

    policy_lse = ppk + jnp.log(pt)
    frozen_lse = fpk + jnp.log(ft)
    gap_mean = gap / pt
    divergence = gap_mean - policy_lse + frozen_lse
    objective, slope = surrogate(picked - policy_lse, beh[...], sgn[...], siz[...])
    weight = msk[...].astype(f32)
    loss[...] = jnp.sum(weight * (objective + kl_weight * divergence), axis=1, keepdims=True)
    rows[1:2, :] = policy_lse
    rows[2:3, :] = gap_mean
    rows[3:4, :] = slope
    rows[4:5, :] = loss_scale * weight
    for b in range(tokens // block_rows):
        span = pl.ds(b * block_rows, block_rows)
        cols[span, :] = rows[:, span].T
        pol, fro = pl_acc[span, :], fl_acc[span, :]
        prob = jnp.exp(pol - cols[span, 1:2])
        value = cols[span, 4:5] * (
            cols[span, 3:4] * (chosen_of(span).astype(f32) - prob)
            + kl_weight * prob * ((pol - fro) - cols[span, 2:3])
        )
        grad[pl.ds(b * 4, 4)] = value.astype(bf16).reshape(4, 2, 16, vocab_rows)

    def product(core, q):
        left = grad[:, core].reshape(tokens // 2, vocab_rows)
        right = pw[:, q * quarter : (q + 1) * quarter]
        made = jnp.dot(left, right, preferred_element_type=f32)
        return made.reshape(4, 2, 2, 16, quarter)

    def sib_copy(q):
        return put(sib_out.at[q], sib_in.at[q], sib_send.at[q], sib_recv.at[q], sibling)

    for q in range(4):
        sib_out[q] = product(1 - c, q).astype(bf16)
        sib_copy(q).start()

    flip_x, flip_y = dev(z, y, 1 - x, c), dev(z, 1 - y, x, c)

    def sides(q):
        order = SCATTER[q]
        own, other = (y, x) if order[0] == "y" else (x, y)
        to_first, to_other = (flip_y, flip_x) if order[0] == "y" else (flip_x, flip_y)
        return own, other, to_first, to_other

    def s1_copy(q, zz):
        _, _, to_first, _ = sides(q)
        return put(s1.at[q, zz], r1.at[q, zz], s1_send.at[q, zz], s1_recv.at[q, zz], to_first)

    def s2_copy(q, zz):
        _, _, _, to_other = sides(q)
        return put(s2.at[q, zz], r2.at[q, zz], s2_send.at[q, zz], s2_recv.at[q, zz], to_other)

    def z_slot(ref, q, way, dest):
        if SCATTER[q][2] == "z":
            return ref.at[q, way, dest, 0]
        return ref.at[q, way, dest]

    def z_copy(q, way, dest):
        where = dev(z + 1, y, x, c) if way == 0 else dev(z - 1, y, x, c)
        return put(
            z_slot(zs, q, way, dest), z_slot(zr, q, way, dest),
            z_send.at[q, way, dest], z_recv.at[q, way, dest], where,
        )

    for q in range(4):
        made = product(c, q)
        sib_copy(q).wait_recv()
        made = made + sib_in[q].astype(f32)
        own, other, _, _ = sides(q)
        for i in range(2):
            for j in range(2):
                acc[q, :, i, j] = made[:, i, j] if SCATTER[q][0] == "y" else made[:, j, i]
        for zz in range(4):
            s1[q, zz] = acc[q, zz, 1 - own].astype(bf16)
            s1_copy(q, zz).start()

    def take_first(q, zz):
        own, _, _, _ = sides(q)
        s1_copy(q, zz).wait_recv()
        acc[q, zz, own] += r1[q, zz].astype(f32)

    for zz in range(4):
        for q in range(4):
            own, other, _, _ = sides(q)
            take_first(q, zz)
            if SCATTER[q][2] == "z":
                s2[q, zz] = acc[q, zz, own, 1 - other].astype(bf16)
                s2_copy(q, zz).start()

    def line_value(q, dest):
        own, other, _, _ = sides(q)
        if SCATTER[q][2] == "z":
            return acc.at[q, dest, own, other]
        return acc.at[q, dest, own]

    def line_step(q, k):
        @pl.when(z + k <= 3)
        def _():
            dest = z + k
            held = line_value(q, dest)

            @pl.when(z > 0)
            def _():
                z_copy(q, 0, dest).wait_recv()
                held[...] += z_slot(zr, q, 0, dest)[...].astype(f32)

            z_slot(zs, q, 0, dest)[...] = held[...].astype(bf16)
            z_copy(q, 0, dest).start()

        @pl.when(z - k >= 0)
        def _():
            dest = z - k
            held = line_value(q, dest)

            @pl.when(z < 3)
            def _():
                z_copy(q, 1, dest).wait_recv()
                held[...] += z_slot(zr, q, 1, dest)[...].astype(f32)

            z_slot(zs, q, 1, dest)[...] = held[...].astype(bf16)
            z_copy(q, 1, dest).start()

    def line_end(q):
        held = line_value(q, z)

        @pl.when(z > 0)
        def _():
            z_copy(q, 0, z).wait_recv()
            held[...] += z_slot(zr, q, 0, z)[...].astype(f32)

        @pl.when(z < 3)
        def _():
            z_copy(q, 1, z).wait_recv()
            held[...] += z_slot(zr, q, 1, z)[...].astype(f32)

    for k in (3, 2, 1):
        for q in (2, 3):
            line_step(q, k)
    for q in (2, 3):
        line_end(q)
        own, other, _, _ = sides(q)
        s2[q, 0] = acc[q, z, own, 1 - other].astype(bf16)
        s2_copy(q, 0).start()
    for q in (0, 1):
        own, other, _, _ = sides(q)
        for zz in range(4):
            s2_copy(q, zz).wait_recv()
            acc[q, zz, own, other] += r2[q, zz].astype(f32)
    for k in (3, 2, 1):
        for q in (0, 1):
            line_step(q, k)
    for q in (2, 3):
        own, other, _, _ = sides(q)
        s2_copy(q, 0).wait_recv()
        done = acc[q, z, own, other] + r2[q, 0].astype(f32)
        out[:, q * quarter : (q + 1) * quarter] = done.astype(bf16)
    for q in (0, 1):
        own, other, _, _ = sides(q)
        line_end(q)
        out[:, q * quarter : (q + 1) * quarter] = acc[q, z, own, other].astype(bf16)

    for k in range(1, 8):
        st1_copy(k, plane).wait_send()
    for k in range(1, 4):
        st2_copy(k, z).wait_send()
    for q in range(4):
        sib_copy(q).wait_send()
        for zz in range(4):
            s1_copy(q, zz).wait_send()
        for zz in range(4 if SCATTER[q][2] == "z" else 1):
            s2_copy(q, zz).wait_send()
        for k in (3, 2, 1):
            @pl.when(z + k <= 3)
            def _():
                z_copy(q, 0, z + k).wait_send()

            @pl.when(z - k >= 0)
            def _():
                z_copy(q, 1, z - k).wait_send()


def fused(ph, fh, pw, fw, actions, behavior, sign, size, mask):
    own_rows, width = ph.shape
    vocab_rows = pw.shape[0]
    tokens = actions.shape[0]
    quarter = width // 4
    vmem, dma = pltpu.VMEM, pltpu.SemaphoreType.DMA
    row = lambda a: a.reshape(1, tokens)
    in_vmem = pl.BlockSpec(memory_space=pltpu.VMEM)
    in_hbm = pl.BlockSpec(memory_space=pl.ANY)
    out, loss = pl.pallas_call(
        kernel,
        out_shape=(
            jax.ShapeDtypeStruct((own_rows, width), bf16),
            jax.ShapeDtypeStruct((1, 1), f32),
        ),
        in_specs=[in_vmem, in_vmem, in_hbm, in_hbm] + [in_vmem] * 5,
        out_specs=(in_vmem, in_vmem),
        scratch_shapes=[
            vmem((2, 4, 2, 2, 2, own_rows, width), bf16),
            vmem((vocab_rows, width), bf16),
            vmem((vocab_rows, width), bf16),
            vmem((tokens, vocab_rows), f32),
            vmem((tokens, vocab_rows), f32),
            vmem((tokens, 128), f32),
            vmem((128, tokens), f32),
            vmem((16, 2, own_rows, vocab_rows), bf16),
            vmem((8, 8, tokens), f32),
            vmem((4, 8, tokens), f32),
            vmem((4, 4, 2, 2, own_rows, quarter), bf16),
            vmem((4, 4, 2, 2, own_rows, quarter), bf16),
            vmem((4, 4, 2, 2, own_rows, quarter), f32),
            vmem((4, 4, 2, own_rows, quarter), bf16),
            vmem((4, 4, 2, own_rows, quarter), bf16),
            vmem((4, 4, own_rows, quarter), bf16),
            vmem((4, 4, own_rows, quarter), bf16),
            vmem((4, 2, 4, 2, own_rows, quarter), bf16),
            vmem((4, 2, 4, 2, own_rows, quarter), bf16),
            dma((2,)), dma((4, 16, 5)), dma((4, 16)), dma((4, 16)),
            dma((8,)), dma((8,)), dma((4,)), dma((4,)),
            dma((4,)), dma((4,)), dma((4, 4)), dma((4, 4)),
            dma((4, 4)), dma((4, 4)), dma((4, 2, 4)), dma((4, 2, 4)),
        ],
        compiler_params=pltpu.CompilerParams(
            collective_id=0, has_side_effects=True, vmem_limit_bytes=60 * 1024 * 1024
        ),
        cost_estimate=pl.CostEstimate(
            flops=6 * tokens * width * vocab_rows,
            bytes_accessed=4 * width * vocab_rows,
            transcendentals=3 * tokens * vocab_rows,
        ),
        name="fused",
    )(ph, fh, pw, fw, row(actions), row(behavior), row(sign), row(size), row(mask))
    return out, loss.reshape(1)


def solution(mesh):
    placed = (
        P(("groups", "vocab"), None),
        P(("groups", "vocab"), None),
        P("vocab", None),
        P("vocab", None),
        P("groups"),
        P("groups"),
        P("groups"),
        P("groups"),
        P("groups"),
    )
    body = fused if dict(mesh.shape) == {"groups": 1, "vocab": 32} else shards
    return jax.shard_map(
        body,
        mesh=mesh,
        in_specs=placed,
        out_specs=(P(("groups", "vocab"), None), P("groups")),
        check_vma=False,
    )
```

```python
import jax
import jax.numpy as jnp
from jax import lax
from jax.experimental import pallas as pl
from jax.experimental.pallas import tpu as pltpu
from jax.sharding import PartitionSpec as P

clip_eps = 0.2
dual_bound = 3.0
kl_weight = 0.1
loss_scale = 16.0


def head_product(rows_block, head):
    return lax.dot_general(
        rows_block, head, (((1,), (1,)), ((), ())), preferred_element_type=jnp.float32
    )


def surrogate(picked_logp, behavior_logprob, advantage_sign, advantage_size):
    advantage = (2 * advantage_sign - 1).astype(jnp.float32) * advantage_size
    ratio = jnp.exp(picked_logp - behavior_logprob)
    clipped = jnp.clip(ratio, 1.0 - clip_eps, 1.0 + clip_eps)
    primary = jnp.maximum(-advantage * ratio, -advantage * clipped)
    objective = jnp.where(advantage < 0, jnp.minimum(primary, -dual_bound * advantage), primary)
    upward = (advantage > 0) & (ratio <= 1.0 + clip_eps)
    downward = (advantage < 0) & (ratio >= 1.0 - clip_eps) & (ratio <= dual_bound)
    slope = jnp.where(upward | downward, -advantage * ratio, jnp.zeros_like(ratio))
    return (objective, slope)


def local_sums(policy_logits, frozen_logits, policy_peak, frozen_peak, chosen):
    policy_exp = jnp.exp(policy_logits - policy_peak[:, None])
    policy_total = jnp.sum(policy_exp, axis=1)
    gap_total = jnp.sum(policy_exp * (policy_logits - frozen_logits), axis=1)
    frozen_total = jnp.sum(jnp.exp(frozen_logits - frozen_peak[:, None]), axis=1)
    picked = jnp.sum(jnp.where(chosen, policy_logits, jnp.zeros_like(policy_logits)), axis=1)
    return (policy_total, gap_total, frozen_total, picked)


def shards(
    policy_hidden,
    frozen_hidden,
    policy_head,
    frozen_head,
    actions,
    behavior_logprob,
    advantage_sign,
    advantage_size,
    response_mask,
):
    own_rows = policy_hidden.shape[0]
    vocab_rows = policy_head.shape[0]
    policy_all, frozen_all = (
        lax.all_gather(policy_hidden, "vocab", axis=0, tiled=True),
        lax.all_gather(frozen_hidden, "vocab", axis=0, tiled=True),
    )
    policy_logits = head_product(policy_all, policy_head)
    frozen_logits = head_product(frozen_all, frozen_head)
    offset = lax.axis_index("vocab") * vocab_rows
    columns = offset + jnp.arange(vocab_rows, dtype=jnp.int32)
    chosen = actions[:, None] == columns[None, :]
    policy_local = jnp.max(policy_logits, axis=1)
    frozen_local = jnp.max(frozen_logits, axis=1)
    policy_peak, frozen_peak = lax.pmax((policy_local, frozen_local), "vocab")
    sums_here = local_sums(policy_logits, frozen_logits, policy_peak, frozen_peak, chosen)
    policy_total, gap_total, frozen_total, picked = lax.psum(
        (sums_here[0], sums_here[1], sums_here[2], sums_here[3]), "vocab"
    )
    policy_lse = policy_peak + jnp.log(policy_total)
    frozen_lse = frozen_peak + jnp.log(frozen_total)
    divergence = gap_total / policy_total - policy_lse + frozen_lse
    objective, slope = surrogate(
        picked - policy_lse, behavior_logprob, advantage_sign, advantage_size
    )
    weight = response_mask.astype(jnp.float32)
    surrogate_loss = jnp.sum(weight * (objective + kl_weight * divergence)).reshape(1)
    policy_prob = jnp.exp(policy_logits - policy_lse[:, None])
    log_gap = policy_logits - frozen_logits - policy_lse[:, None] + frozen_lse[:, None]
    logit_grad = (loss_scale * weight)[:, None] * (
        slope[:, None] * (chosen.astype(jnp.float32) - policy_prob)
        + kl_weight * policy_prob * (log_gap - divergence[:, None])
    )
    logit_grad = logit_grad.astype(jnp.bfloat16)
    partial_grad = jnp.dot(logit_grad, policy_head, preferred_element_type=jnp.float32)
    summed = lax.psum(partial_grad, "vocab")
    hidden_grad = lax.dynamic_slice_in_dim(summed, lax.axis_index("vocab") * own_rows, own_rows, 0)
    return (hidden_grad.astype(jnp.bfloat16), surrogate_loss)


MESH = pl.DeviceIdType.MESH
f32 = jnp.float32
bf16 = jnp.bfloat16
GATHER = ((0, 0, "zxy"), (0, 1, "zyx"), (1, 0, "xzy"), (1, 1, "yzx"))
SCATTER = ("yxz", "xyz", "yzx", "xzy")


def nt_dot(a, b):
    return lax.dot_general(a, b, (((1,), (1,)), ((), ())), preferred_element_type=f32)


def gather_events():
    events = []
    for part, (_, _, order) in enumerate(GATHER):
        for dz in range(-3, 4):
            for dy in range(2):
                for dx in range(2):
                    moved = {"z": dz, "y": dy, "x": dx}
                    last = max([order.index(a) for a in order if moved[a]], default=-1)
                    onward = order[last + 1 :]
                    depth = abs(dz) + dy + dx
                    late = moved[order[2]]
                    events.append((depth, part, dz, dy, dx, order[last] if last >= 0 else "", onward, late))
    events.sort(key=lambda e: (e[0], e[7], e[1]))
    return events


def kernel(
    ph, fh, pw_hbm, fw_hbm, act, beh, sgn, siz, msk,
    out, loss,
    hid, pw, fw, pl_acc, fl_acc, cols, rows, grad, st1, st2,
    sib_out, sib_in, acc, s1, r1, s2, r2, zs, zr,
    load_sem, g_send, g_recv, g_sib, st_send, st_recv, st2_send, st2_recv,
    sib_send, sib_recv, s1_send, s1_recv, s2_send, s2_recv, z_send, z_recv,
):
    tokens, vocab_rows = cols.shape[0], pw.shape[0]
    width = ph.shape[1]
    half, quarter = width // 2, width // 4
    me = lax.axis_index("vocab")
    c, x, y, z = me % 2, (me // 2) % 2, (me // 4) % 2, me // 8
    plane = me % 8

    def dev(zz, yy, xx, cc):
        return {"vocab": ((zz * 2 + yy) * 2 + xx) * 2 + cc}

    sibling = dev(z, y, x, 1 - c)

    def put(src, dst, send, recv, where):
        return pltpu.make_async_remote_copy(
            src_ref=src, dst_ref=dst, send_sem=send, recv_sem=recv,
            device_id=where, device_id_type=MESH,
        )

    load_p = pltpu.make_async_copy(pw_hbm, pw, load_sem.at[0])
    load_f = pltpu.make_async_copy(fw_hbm, fw, load_sem.at[1])
    load_p.start()
    load_f.start()
    barrier = pltpu.get_barrier_semaphore()
    for k in range(1, 8):
        pl.semaphore_signal(
            barrier, inc=1, device_id={"vocab": z * 8 + (plane + k) % 8}, device_id_type=MESH
        )
    for k in range(1, 4):
        pl.semaphore_signal(
            barrier, inc=1, device_id={"vocab": ((z + k) % 4) * 8 + plane}, device_id_type=MESH
        )
    pl_acc[...] = jnp.zeros_like(pl_acc)
    fl_acc[...] = jnp.zeros_like(fl_acc)
    hid[0, z, y, x, c] = ph[...]
    hid[1, z, y, x, c] = fh[...]
    pl.semaphore_wait(barrier, 10)

    def chunk(part, sz, sy, sx, sc):
        model, side, _ = GATHER[part]
        return hid.at[model, sz, sy, sx, sc, :, pl.ds(side * half, half)]

    def gather_copy(part, sz, sy, sx, way):
        where, slot = {
            "+": (dev(z + 1, y, x, c), 0),
            "-": (dev(z - 1, y, x, c), 1),
            "y": (dev(z, 1 - y, x, c), 2),
            "x": (dev(z, y, 1 - x, c), 3),
            "s": (sibling, 4),
        }[way]
        source = (sz * 2 + sy) * 2 + sx
        block = chunk(part, sz, sy, sx, c)
        if way == "s":
            _, _, order = GATHER[part]
            recv = g_sib.at[part, source]
        else:
            recv = g_recv.at[part, source]
        return put(block, block, g_send.at[part, source, slot], recv, where)

    def gather_event(event, act_on):
        _, part, dz, dy, dx, last, onward, _ = event
        sz, sy, sx = z + dz, (1 - y if dy else y), (1 - x if dx else x)

        def go():
            if act_on == "start" and last:
                gather_copy(part, sz, sy, sx, "y").wait_recv()

            def each(way, cond=None):
                def run():
                    copy = gather_copy(part, sz, sy, sx, way)
                    if act_on == "start":
                        copy.start()
                    else:
                        copy.wait_send()

                if cond is None:
                    run()
                else:
                    pl.when(cond)(run)

            if ("z" in onward and dz == 0) or (last == "z" and dz < 0):
                each("+", z < 3)
            if ("z" in onward and dz == 0) or (last == "z" and dz > 0):
                each("-", z > 0)
            for way in onward:
                if way != "z":
                    each(way)
            each("s")

        if dz == 0:
            go()
        else:
            pl.when((sz >= 0) & (sz <= 3))(go)

    def wait_sibling(part, far):
        _, _, order = GATHER[part]

        @pl.loop(0, 8)
        def _(i):
            sz, j = i // 2, i % 2
            if order[2] == "y":
                sy, sx = (1 - y if far else y), j
            else:
                sy, sx = j, (1 - x if far else x)
            block = chunk(part, sz, sy, sx, 1 - c)
            source = (sz * 2 + sy) * 2 + sx
            put(block, block, g_send.at[part, 0, 4], g_sib.at[part, source], sibling).wait_recv()

    tile = half // 2

    def logits_piece(part, far, i):
        model, side, order = GATHER[part]
        head, total = (pw, pl_acc) if model == 0 else (fw, fl_acc)
        span = pl.ds(side * half + i * tile, tile)
        shape = (4, 2, 2, 16, vocab_rows)
        if order[2] == "y":
            at = 1 - y if far else y
            left = hid[model, :, at, :, :, :, span].reshape(tokens // 2, tile)
            total[:, at] += nt_dot(left, head[:, span]).reshape(shape)
        else:
            at = 1 - x if far else x
            left = hid[model, :, :, at, :, :, span].reshape(tokens // 2, tile)
            total[:, :, at] += nt_dot(left, head[:, span]).reshape(shape)

    events = gather_events()
    cut = max(i for i, e in enumerate(events) if not e[7]) + 1
    for event in events[:cut]:
        gather_event(event, "start")
        if event[0] == 0 and event[1] == 3:
            rows[...] = jnp.zeros_like(rows)
            rows[0:1, :] = act[...].astype(f32)
            for b in range(tokens // 128):
                span = pl.ds(b * 128, 128)
                cols[span, :] = rows[:, span].T
    load_p.wait()
    load_f.wait()
    left_over = events[cut:]
    pieces = [(part, i) for part in range(4) for i in range(2)]
    step = -(-len(left_over) // len(pieces))
    for n, (part, i) in enumerate(pieces):
        if i == 0:
            wait_sibling(part, False)
        logits_piece(part, False, i)
        for event in left_over[n * step : (n + 1) * step]:
            gather_event(event, "start")
    for part, i in pieces:
        if i == 0:
            wait_sibling(part, True)
        logits_piece(part, True, i)

    block_rows = 128
    first = (me * vocab_rows).astype(f32)

    def chosen_of(span):
        ids = lax.broadcasted_iota(jnp.int32, (block_rows, vocab_rows), 1).astype(f32) + first
        return cols[span, 0:1] == ids

    for b in range(tokens // block_rows):
        span = pl.ds(b * block_rows, block_rows)
        pol = pl_acc[b].reshape(block_rows, vocab_rows)
        fro = fl_acc[b].reshape(block_rows, vocab_rows)
        ppk = jnp.max(pol, axis=1, keepdims=True)
        fpk = jnp.max(fro, axis=1, keepdims=True)
        ex = jnp.exp(pol - ppk)
        stats = (
            ppk,
            jnp.sum(ex, axis=1, keepdims=True),
            jnp.sum(ex * (pol - fro), axis=1, keepdims=True),
            fpk,
            jnp.sum(jnp.exp(fro - fpk), axis=1, keepdims=True),
            jnp.sum(jnp.where(chosen_of(span), pol, 0.0), axis=1, keepdims=True),
        )
        lane = lax.broadcasted_iota(jnp.int32, (block_rows, 128), 1)
        packed = jnp.zeros((block_rows, 128), f32)
        for i, s in enumerate(stats):
            packed = jnp.where(lane == i, s, packed)
        st1[plane, :, b * block_rows : (b + 1) * block_rows] = packed.T[0:8, :]

    def combine(blocks):
        ppk, fpk = blocks[0][0:1], blocks[0][3:4]
        for blk in blocks[1:]:
            ppk, fpk = jnp.maximum(ppk, blk[0:1]), jnp.maximum(fpk, blk[3:4])
        pt = gap = ft = pick = 0.0
        for blk in blocks:
            scale = jnp.exp(blk[0:1] - ppk)
            pt = pt + scale * blk[1:2]
            gap = gap + scale * blk[2:3]
            ft = ft + jnp.exp(blk[3:4] - fpk) * blk[4:5]
            pick = pick + blk[5:6]
        return ppk, pt, gap, fpk, ft, pick

    def st1_copy(k, slot):
        where = {"vocab": z * 8 + (plane + k) % 8}
        return put(st1.at[slot], st1.at[slot], st_send.at[k], st_recv.at[slot], where)

    def st2_copy(k, slot):
        where = {"vocab": ((z + k) % 4) * 8 + plane}
        return put(st2.at[slot], st2.at[slot], st2_send.at[k], st2_recv.at[slot], where)

    for k in range(1, 8):
        st1_copy(k, plane).start()
    for event in events:
        gather_event(event, "finish")
    for k in range(1, 8):
        st1_copy(k, (plane + k) % 8).wait_recv()
    both = combine([st1[i] for i in range(8)])
    for i, s in enumerate(both):
        st2[z, i : i + 1, :] = s
    st2[z, 6:8, :] = jnp.zeros((2, tokens), f32)
    for k in range(1, 4):
        st2_copy(k, z).start()
    for k in range(1, 4):
        st2_copy(k, (z + k) % 4).wait_recv()
    ppk, pt, gap, fpk, ft, picked = combine([st2[i] for i in range(4)])

    policy_lse = ppk + jnp.log(pt)
    frozen_lse = fpk + jnp.log(ft)
    gap_mean = gap / pt
    divergence = gap_mean - policy_lse + frozen_lse
    objective, slope = surrogate(picked - policy_lse, beh[...], sgn[...], siz[...])
    weight = msk[...].astype(f32)
    loss[...] = jnp.sum(weight * (objective + kl_weight * divergence), axis=1, keepdims=True)
    rows[1:2, :] = policy_lse
    rows[2:3, :] = gap_mean
    rows[3:4, :] = slope
    rows[4:5, :] = loss_scale * weight
    for b in range(tokens // block_rows):
        span = pl.ds(b * block_rows, block_rows)
        cols[span, :] = rows[:, span].T
        pol = pl_acc[b].reshape(block_rows, vocab_rows)
        fro = fl_acc[b].reshape(block_rows, vocab_rows)
        prob = jnp.exp(pol - cols[span, 1:2])
        value = cols[span, 4:5] * (
            cols[span, 3:4] * (chosen_of(span).astype(f32) - prob)
            + kl_weight * prob * ((pol - fro) - cols[span, 2:3])
        )
        grad[pl.ds(b * 4, 4)] = value.astype(bf16).reshape(4, 2, 16, vocab_rows)

    def product(core, q):
        left = grad[:, core].reshape(tokens // 2, vocab_rows)
        right = pw[:, q * quarter : (q + 1) * quarter]
        made = jnp.dot(left, right, preferred_element_type=f32)
        return made.reshape(4, 2, 2, 16, quarter)

    def sib_copy(q):
        return put(sib_out.at[q], sib_in.at[q], sib_send.at[q], sib_recv.at[q], sibling)

    def for_sibling(q):
        sib_out[q] = product(1 - c, q).astype(bf16)
        sib_copy(q).start()

    flip_x, flip_y = dev(z, y, 1 - x, c), dev(z, 1 - y, x, c)

    def sides(q):
        order = SCATTER[q]
        own, other = (y, x) if order[0] == "y" else (x, y)
        to_first, to_other = (flip_y, flip_x) if order[0] == "y" else (flip_x, flip_y)
        return own, other, to_first, to_other

    def s1_copy(q, zz):
        _, _, to_first, _ = sides(q)
        return put(s1.at[q, zz], r1.at[q, zz], s1_send.at[q, zz], s1_recv.at[q, zz], to_first)

    def s2_copy(q, zz):
        _, _, _, to_other = sides(q)
        return put(s2.at[q, zz], r2.at[q, zz], s2_send.at[q, zz], s2_recv.at[q, zz], to_other)

    def z_slot(ref, q, way, dest):
        return ref.at[q, way, dest]

    def z_copy(q, way, dest):
        where = dev(z + 1, y, x, c) if way == 0 else dev(z - 1, y, x, c)
        return put(
            z_slot(zs, q, way, dest), z_slot(zr, q, way, dest),
            z_send.at[q, way, dest], z_recv.at[q, way, dest], where,
        )

    def for_own(q):
        made = product(c, q)
        sib_copy(q).wait_recv()
        made = made + sib_in[q].astype(f32)
        own, other, _, _ = sides(q)
        for i in range(2):
            for j in range(2):
                acc[q, :, i, j] = made[:, i, j] if SCATTER[q][0] == "y" else made[:, j, i]
        for zz in range(4):
            s1[q, zz] = acc[q, zz, 1 - own].astype(bf16)
            s1_copy(q, zz).start()

    for_sibling(2)
    for_sibling(3)
    for_own(2)
    for_sibling(0)
    for_own(3)
    for_sibling(1)
    for_own(0)
    for_own(1)

    def take_first(q, zz):
        own, other, _, _ = sides(q)
        s1_copy(q, zz).wait_recv()
        acc[q, zz, own] += r1[q, zz].astype(f32)
        if SCATTER[q][2] == "z":
            s2[q, zz] = acc[q, zz, own, 1 - other].astype(bf16)
            s2_copy(q, zz).start()

    def line_value(q, dest):
        own, _, _, _ = sides(q)
        return acc.at[q, dest, own]

    def line_step(q, k):
        @pl.when(z + k <= 3)
        def _():
            dest = z + k
            held = line_value(q, dest)

            @pl.when(z > 0)
            def _():
                z_copy(q, 0, dest).wait_recv()
                held[...] += z_slot(zr, q, 0, dest)[...].astype(f32)

            z_slot(zs, q, 0, dest)[...] = held[...].astype(bf16)
            z_copy(q, 0, dest).start()

        @pl.when(z - k >= 0)
        def _():
            dest = z - k
            held = line_value(q, dest)

            @pl.when(z < 3)
            def _():
                z_copy(q, 1, dest).wait_recv()
                held[...] += z_slot(zr, q, 1, dest)[...].astype(f32)

            z_slot(zs, q, 1, dest)[...] = held[...].astype(bf16)
            z_copy(q, 1, dest).start()

    def line_end(q):
        held = line_value(q, z)

        @pl.when(z > 0)
        def _():
            z_copy(q, 0, z).wait_recv()
            held[...] += z_slot(zr, q, 0, z)[...].astype(f32)

        @pl.when(z < 3)
        def _():
            z_copy(q, 1, z).wait_recv()
            held[...] += z_slot(zr, q, 1, z)[...].astype(f32)

    def direct_copy(q, dest, slot):
        return put(
            zs.at[q, 0, dest, 0], zr.at[q, 0, slot, 0],
            z_send.at[q, 0, dest], z_recv.at[q, 0, slot], dev(dest, y, x, c),
        )

    for zz in range(4):
        for q in (2, 3):
            take_first(q, zz)
    for k in (3, 2, 1):
        for q in (2, 3):
            line_step(q, k)
        for q in (0, 1):
            take_first(q, 3 - k)
    for q in (2, 3):
        line_end(q)
        own, other, _, _ = sides(q)
        s2[q, 0] = acc[q, z, own, 1 - other].astype(bf16)
        s2_copy(q, 0).start()
    for q in (0, 1):
        take_first(q, 3)
    for zz in range(4):
        for q in (0, 1):
            own, other, _, _ = sides(q)
            s2_copy(q, zz).wait_recv()
            acc[q, zz, own, other] += r2[q, zz].astype(f32)

            @pl.when(z != zz)
            def _():
                zs[q, 0, zz, 0] = acc[q, zz, own, other].astype(bf16)
                direct_copy(q, zz, z).start()

    for q in (2, 3):
        own, other, _, _ = sides(q)
        s2_copy(q, 0).wait_recv()
        done = acc[q, z, own, other] + r2[q, 0].astype(f32)
        out[:, q * quarter : (q + 1) * quarter] = done.astype(bf16)
    for q in (0, 1):
        own, other, _, _ = sides(q)
        done = acc[q, z, own, other]
        for k in range(1, 4):
            source = (z + k) % 4
            direct_copy(q, source, source).wait_recv()
            done = done + zr[q, 0, source, 0].astype(f32)
        out[:, q * quarter : (q + 1) * quarter] = done.astype(bf16)

    for k in range(1, 8):
        st1_copy(k, plane).wait_send()
    for k in range(1, 4):
        st2_copy(k, z).wait_send()
    for q in range(4):
        sib_copy(q).wait_send()
        for zz in range(4):
            s1_copy(q, zz).wait_send()
        for zz in range(4 if SCATTER[q][2] == "z" else 1):
            s2_copy(q, zz).wait_send()
        if SCATTER[q][2] == "z":
            for k in range(1, 4):
                direct_copy(q, (z + k) % 4, z).wait_send()
            continue
        for k in (3, 2, 1):
            @pl.when(z + k <= 3)
            def _():
                z_copy(q, 0, z + k).wait_send()

            @pl.when(z - k >= 0)
            def _():
                z_copy(q, 1, z - k).wait_send()


def fused(ph, fh, pw, fw, actions, behavior, sign, size, mask):
    own_rows, width = ph.shape
    vocab_rows = pw.shape[0]
    tokens = actions.shape[0]
    quarter = width // 4
    vmem, dma = pltpu.VMEM, pltpu.SemaphoreType.DMA
    row = lambda a: a.reshape(1, tokens)
    in_vmem = pl.BlockSpec(memory_space=pltpu.VMEM)
    in_hbm = pl.BlockSpec(memory_space=pl.ANY)
    out, loss = pl.pallas_call(
        kernel,
        out_shape=(
            jax.ShapeDtypeStruct((own_rows, width), bf16),
            jax.ShapeDtypeStruct((1, 1), f32),
        ),
        in_specs=[in_vmem, in_vmem, in_hbm, in_hbm] + [in_vmem] * 5,
        out_specs=(in_vmem, in_vmem),
        scratch_shapes=[
            vmem((2, 4, 2, 2, 2, own_rows, width), bf16),
            vmem((vocab_rows, width), bf16),
            vmem((vocab_rows, width), bf16),
            vmem((4, 2, 2, 2, own_rows, vocab_rows), f32),
            vmem((4, 2, 2, 2, own_rows, vocab_rows), f32),
            vmem((tokens, 128), f32),
            vmem((128, tokens), f32),
            vmem((16, 2, own_rows, vocab_rows), bf16),
            vmem((8, 8, tokens), f32),
            vmem((4, 8, tokens), f32),
            vmem((4, 4, 2, 2, own_rows, quarter), bf16),
            vmem((4, 4, 2, 2, own_rows, quarter), bf16),
            vmem((4, 4, 2, 2, own_rows, quarter), f32),
            vmem((4, 4, 2, own_rows, quarter), bf16),
            vmem((4, 4, 2, own_rows, quarter), bf16),
            vmem((4, 4, own_rows, quarter), bf16),
            vmem((4, 4, own_rows, quarter), bf16),
            vmem((4, 2, 4, 2, own_rows, quarter), bf16),
            vmem((4, 2, 4, 2, own_rows, quarter), bf16),
            dma((2,)), dma((4, 16, 5)), dma((4, 16)), dma((4, 16)),
            dma((8,)), dma((8,)), dma((4,)), dma((4,)),
            dma((4,)), dma((4,)), dma((4, 4)), dma((4, 4)),
            dma((4, 4)), dma((4, 4)), dma((4, 2, 4)), dma((4, 2, 4)),
        ],
        compiler_params=pltpu.CompilerParams(
            collective_id=0, has_side_effects=True, vmem_limit_bytes=60 * 1024 * 1024
        ),
        cost_estimate=pl.CostEstimate(
            flops=6 * tokens * width * vocab_rows,
            bytes_accessed=4 * width * vocab_rows,
            transcendentals=3 * tokens * vocab_rows,
        ),
        name="fused",
    )(ph, fh, pw, fw, row(actions), row(behavior), row(sign), row(size), row(mask))
    return out, loss.reshape(1)


def solution(mesh):
    placed = (
        P(("groups", "vocab"), None),
        P(("groups", "vocab"), None),
        P("vocab", None),
        P("vocab", None),
        P("groups"),
        P("groups"),
        P("groups"),
        P("groups"),
        P("groups"),
    )
    body = fused if dict(mesh.shape) == {"groups": 1, "vocab": 32} else shards
    return jax.shard_map(
        body,
        mesh=mesh,
        in_specs=placed,
        out_specs=(P(("groups", "vocab"), None), P("groups")),
        check_vma=False,
    )
```

```python
import jax
import jax.numpy as jnp
from jax import lax
from jax.experimental import pallas as pl
from jax.experimental.pallas import tpu as pltpu
from jax.sharding import PartitionSpec as P

clip_eps = 0.2
dual_bound = 3.0
kl_weight = 0.1
loss_scale = 16.0


def head_product(rows_block, head):
    return lax.dot_general(
        rows_block, head, (((1,), (1,)), ((), ())), preferred_element_type=jnp.float32
    )


def surrogate(picked_logp, behavior_logprob, advantage_sign, advantage_size):
    advantage = (2 * advantage_sign - 1).astype(jnp.float32) * advantage_size
    ratio = jnp.exp(picked_logp - behavior_logprob)
    clipped = jnp.clip(ratio, 1.0 - clip_eps, 1.0 + clip_eps)
    primary = jnp.maximum(-advantage * ratio, -advantage * clipped)
    objective = jnp.where(advantage < 0, jnp.minimum(primary, -dual_bound * advantage), primary)
    upward = (advantage > 0) & (ratio <= 1.0 + clip_eps)
    downward = (advantage < 0) & (ratio >= 1.0 - clip_eps) & (ratio <= dual_bound)
    slope = jnp.where(upward | downward, -advantage * ratio, jnp.zeros_like(ratio))
    return (objective, slope)


def local_sums(policy_logits, frozen_logits, policy_peak, frozen_peak, chosen):
    policy_exp = jnp.exp(policy_logits - policy_peak[:, None])
    policy_total = jnp.sum(policy_exp, axis=1)
    gap_total = jnp.sum(policy_exp * (policy_logits - frozen_logits), axis=1)
    frozen_total = jnp.sum(jnp.exp(frozen_logits - frozen_peak[:, None]), axis=1)
    picked = jnp.sum(jnp.where(chosen, policy_logits, jnp.zeros_like(policy_logits)), axis=1)
    return (policy_total, gap_total, frozen_total, picked)


def shards(
    policy_hidden,
    frozen_hidden,
    policy_head,
    frozen_head,
    actions,
    behavior_logprob,
    advantage_sign,
    advantage_size,
    response_mask,
):
    own_rows = policy_hidden.shape[0]
    vocab_rows = policy_head.shape[0]
    policy_all, frozen_all = (
        lax.all_gather(policy_hidden, "vocab", axis=0, tiled=True),
        lax.all_gather(frozen_hidden, "vocab", axis=0, tiled=True),
    )
    policy_logits = head_product(policy_all, policy_head)
    frozen_logits = head_product(frozen_all, frozen_head)
    offset = lax.axis_index("vocab") * vocab_rows
    columns = offset + jnp.arange(vocab_rows, dtype=jnp.int32)
    chosen = actions[:, None] == columns[None, :]
    policy_local = jnp.max(policy_logits, axis=1)
    frozen_local = jnp.max(frozen_logits, axis=1)
    policy_peak, frozen_peak = lax.pmax((policy_local, frozen_local), "vocab")
    sums_here = local_sums(policy_logits, frozen_logits, policy_peak, frozen_peak, chosen)
    policy_total, gap_total, frozen_total, picked = lax.psum(
        (sums_here[0], sums_here[1], sums_here[2], sums_here[3]), "vocab"
    )
    policy_lse = policy_peak + jnp.log(policy_total)
    frozen_lse = frozen_peak + jnp.log(frozen_total)
    divergence = gap_total / policy_total - policy_lse + frozen_lse
    objective, slope = surrogate(
        picked - policy_lse, behavior_logprob, advantage_sign, advantage_size
    )
    weight = response_mask.astype(jnp.float32)
    surrogate_loss = jnp.sum(weight * (objective + kl_weight * divergence)).reshape(1)
    policy_prob = jnp.exp(policy_logits - policy_lse[:, None])
    log_gap = policy_logits - frozen_logits - policy_lse[:, None] + frozen_lse[:, None]
    logit_grad = (loss_scale * weight)[:, None] * (
        slope[:, None] * (chosen.astype(jnp.float32) - policy_prob)
        + kl_weight * policy_prob * (log_gap - divergence[:, None])
    )
    logit_grad = logit_grad.astype(jnp.bfloat16)
    partial_grad = jnp.dot(logit_grad, policy_head, preferred_element_type=jnp.float32)
    summed = lax.psum(partial_grad, "vocab")
    hidden_grad = lax.dynamic_slice_in_dim(summed, lax.axis_index("vocab") * own_rows, own_rows, 0)
    return (hidden_grad.astype(jnp.bfloat16), surrogate_loss)


MESH = pl.DeviceIdType.MESH
f32 = jnp.float32
bf16 = jnp.bfloat16
GATHER = ((0, 0, "zxy"), (0, 1, "zyx"), (1, 0, "xzy"), (1, 1, "yzx"))
SCATTER = ("yxz", "xyz", "yzx", "xzy")


def nt_dot(a, b):
    return lax.dot_general(a, b, (((1,), (1,)), ((), ())), preferred_element_type=f32)


def gather_events():
    events = []
    for part, (_, _, order) in enumerate(GATHER):
        for dz in range(-3, 4):
            for dy in range(2):
                for dx in range(2):
                    moved = {"z": dz, "y": dy, "x": dx}
                    last = max([order.index(a) for a in order if moved[a]], default=-1)
                    onward = order[last + 1 :]
                    depth = abs(dz) + dy + dx
                    late = moved[order[2]]
                    events.append((depth, part, dz, dy, dx, order[last] if last >= 0 else "", onward, late))
    events.sort(key=lambda e: (e[0], e[7], e[1]))
    return events


def kernel(
    ph, fh, pw_hbm, fw_hbm, act, beh, sgn, siz, msk,
    out, loss,
    hid, pw, fw, pl_acc, fl_acc, cols, rows, grad, st1, st2,
    sib_out, sib_in, acc, s1, r1, s2, r2, zs, zr,
    load_sem, g_send, g_recv, g_sib, st_send, st_recv, st2_send, st2_recv,
    sib_send, sib_recv, s1_send, s1_recv, s2_send, s2_recv, z_send, z_recv,
):
    tokens, vocab_rows = cols.shape[0], pw.shape[0]
    width = ph.shape[1]
    half, quarter = width // 2, width // 4
    me = lax.axis_index("vocab")
    c, x, y, z = me % 2, (me // 2) % 2, (me // 4) % 2, me // 8
    plane = me % 8

    def dev(zz, yy, xx, cc):
        return {"vocab": ((zz * 2 + yy) * 2 + xx) * 2 + cc}

    sibling = dev(z, y, x, 1 - c)

    def put(src, dst, send, recv, where):
        return pltpu.make_async_remote_copy(
            src_ref=src, dst_ref=dst, send_sem=send, recv_sem=recv,
            device_id=where, device_id_type=MESH,
        )

    load_p = pltpu.make_async_copy(pw_hbm, pw, load_sem.at[0])
    load_f = pltpu.make_async_copy(fw_hbm, fw, load_sem.at[1])
    load_p.start()
    load_f.start()
    barrier = pltpu.get_barrier_semaphore()
    for k in range(1, 8):
        pl.semaphore_signal(
            barrier, inc=1, device_id={"vocab": z * 8 + (plane + k) % 8}, device_id_type=MESH
        )
    for k in range(1, 4):
        pl.semaphore_signal(
            barrier, inc=1, device_id={"vocab": ((z + k) % 4) * 8 + plane}, device_id_type=MESH
        )
    pl_acc[...] = jnp.zeros_like(pl_acc)
    fl_acc[...] = jnp.zeros_like(fl_acc)
    hid[0, z, y, x, c] = ph[...]
    hid[1, z, y, x, c] = fh[...]
    pl.semaphore_wait(barrier, 10)

    def chunk(part, sz, sy, sx, sc):
        model, side, _ = GATHER[part]
        return hid.at[model, sz, sy, sx, sc, :, pl.ds(side * half, half)]

    def gather_copy(part, sz, sy, sx, way):
        where, slot = {
            "+": (dev(z + 1, y, x, c), 0),
            "-": (dev(z - 1, y, x, c), 1),
            "y": (dev(z, 1 - y, x, c), 2),
            "x": (dev(z, y, 1 - x, c), 3),
            "s": (sibling, 4),
        }[way]
        source = (sz * 2 + sy) * 2 + sx
        block = chunk(part, sz, sy, sx, c)
        if way == "s":
            _, _, order = GATHER[part]
            recv = g_sib.at[part, source]
        else:
            recv = g_recv.at[part, source]
        return put(block, block, g_send.at[part, source, slot], recv, where)

    def gather_event(event, act_on):
        _, part, dz, dy, dx, last, onward, _ = event
        sz, sy, sx = z + dz, (1 - y if dy else y), (1 - x if dx else x)

        def go():
            if act_on == "start" and last:
                gather_copy(part, sz, sy, sx, "y").wait_recv()

            def each(way, cond=None):
                def run():
                    copy = gather_copy(part, sz, sy, sx, way)
                    if act_on == "start":
                        copy.start()
                    else:
                        copy.wait_send()

                if cond is None:
                    run()
                else:
                    pl.when(cond)(run)

            if ("z" in onward and dz == 0) or (last == "z" and dz < 0):
                each("+", z < 3)
            if ("z" in onward and dz == 0) or (last == "z" and dz > 0):
                each("-", z > 0)
            for way in onward:
                if way != "z":
                    each(way)
            each("s")

        if dz == 0:
            go()
        else:
            pl.when((sz >= 0) & (sz <= 3))(go)

    def wait_sibling(part, far):
        _, _, order = GATHER[part]

        @pl.loop(0, 8)
        def _(i):
            sz, j = i // 2, i % 2
            if order[2] == "y":
                sy, sx = (1 - y if far else y), j
            else:
                sy, sx = j, (1 - x if far else x)
            block = chunk(part, sz, sy, sx, 1 - c)
            source = (sz * 2 + sy) * 2 + sx
            put(block, block, g_send.at[part, 0, 4], g_sib.at[part, source], sibling).wait_recv()

    tile = half // 2

    def logits_piece(part, far, i):
        model, side, order = GATHER[part]
        head, total = (pw, pl_acc) if model == 0 else (fw, fl_acc)
        span = pl.ds(side * half + i * tile, tile)
        shape = (4, 2, 2, 16, vocab_rows)
        if order[2] == "y":
            at = 1 - y if far else y
            left = hid[model, :, at, :, :, :, span].reshape(tokens // 2, tile)
            total[:, at] += nt_dot(left, head[:, span]).reshape(shape)
        else:
            at = 1 - x if far else x
            left = hid[model, :, :, at, :, :, span].reshape(tokens // 2, tile)
            total[:, :, at] += nt_dot(left, head[:, span]).reshape(shape)

    events = gather_events()
    cut = max(i for i, e in enumerate(events) if not e[7]) + 1
    for event in events[:cut]:
        gather_event(event, "start")
        if event[0] == 0 and event[1] == 3:
            rows[...] = jnp.zeros_like(rows)
            rows[0:1, :] = act[...].astype(f32)
            for b in range(tokens // 128):
                span = pl.ds(b * 128, 128)
                cols[span, :] = rows[:, span].T
    load_p.wait()
    load_f.wait()
    left_over = events[cut:]
    pieces = [(part, i) for part in range(4) for i in range(2)]
    step = -(-len(left_over) // len(pieces))
    for n, (part, i) in enumerate(pieces):
        if i == 0:
            wait_sibling(part, False)
        logits_piece(part, False, i)
        for event in left_over[n * step : (n + 1) * step]:
            gather_event(event, "start")
    for part, i in pieces:
        if i == 0:
            wait_sibling(part, True)
        logits_piece(part, True, i)

    block_rows = 128
    first = (me * vocab_rows).astype(f32)

    def chosen_of(span):
        ids = lax.broadcasted_iota(jnp.int32, (block_rows, vocab_rows), 1).astype(f32) + first
        return cols[span, 0:1] == ids

    for b in range(tokens // block_rows):
        span = pl.ds(b * block_rows, block_rows)
        pol = pl_acc[b].reshape(block_rows, vocab_rows)
        fro = fl_acc[b].reshape(block_rows, vocab_rows)
        ppk = jnp.max(pol, axis=1, keepdims=True)
        fpk = jnp.max(fro, axis=1, keepdims=True)
        ex = jnp.exp(pol - ppk)
        stats = (
            ppk,
            jnp.sum(ex, axis=1, keepdims=True),
            jnp.sum(ex * (pol - fro), axis=1, keepdims=True),
            fpk,
            jnp.sum(jnp.exp(fro - fpk), axis=1, keepdims=True),
            jnp.sum(jnp.where(chosen_of(span), pol, 0.0), axis=1, keepdims=True),
        )
        lane = lax.broadcasted_iota(jnp.int32, (block_rows, 128), 1)
        packed = jnp.zeros((block_rows, 128), f32)
        for i, s in enumerate(stats):
            packed = jnp.where(lane == i, s, packed)
        st1[plane, :, b * block_rows : (b + 1) * block_rows] = packed.T[0:8, :]

    def combine(blocks):
        ppk, fpk = blocks[0][0:1], blocks[0][3:4]
        for blk in blocks[1:]:
            ppk, fpk = jnp.maximum(ppk, blk[0:1]), jnp.maximum(fpk, blk[3:4])
        pt = gap = ft = pick = 0.0
        for blk in blocks:
            scale = jnp.exp(blk[0:1] - ppk)
            pt = pt + scale * blk[1:2]
            gap = gap + scale * blk[2:3]
            ft = ft + jnp.exp(blk[3:4] - fpk) * blk[4:5]
            pick = pick + blk[5:6]
        return ppk, pt, gap, fpk, ft, pick

    def st1_copy(k, slot):
        where = {"vocab": z * 8 + (plane + k) % 8}
        return put(st1.at[slot], st1.at[slot], st_send.at[k], st_recv.at[slot], where)

    def st2_copy(k, slot):
        where = {"vocab": ((z + k) % 4) * 8 + plane}
        return put(st2.at[slot], st2.at[slot], st2_send.at[k], st2_recv.at[slot], where)

    for k in range(1, 8):
        st1_copy(k, plane).start()
    for event in events:
        gather_event(event, "finish")
    for k in range(1, 8):
        st1_copy(k, (plane + k) % 8).wait_recv()
    both = combine([st1[i] for i in range(8)])
    for i, s in enumerate(both):
        st2[z, i : i + 1, :] = s
    st2[z, 6:8, :] = jnp.zeros((2, tokens), f32)
    for k in range(1, 4):
        st2_copy(k, z).start()
    for k in range(1, 4):
        st2_copy(k, (z + k) % 4).wait_recv()
    ppk, pt, gap, fpk, ft, picked = combine([st2[i] for i in range(4)])

    policy_lse = ppk + jnp.log(pt)
    frozen_lse = fpk + jnp.log(ft)
    gap_mean = gap / pt
    divergence = gap_mean - policy_lse + frozen_lse
    objective, slope = surrogate(picked - policy_lse, beh[...], sgn[...], siz[...])
    weight = msk[...].astype(f32)
    loss[...] = jnp.sum(weight * (objective + kl_weight * divergence), axis=1, keepdims=True)
    rows[1:2, :] = policy_lse
    rows[2:3, :] = gap_mean
    rows[3:4, :] = slope
    rows[4:5, :] = loss_scale * weight
    for b in range(tokens // block_rows):
        span = pl.ds(b * block_rows, block_rows)
        cols[span, :] = rows[:, span].T
        pol = pl_acc[b].reshape(block_rows, vocab_rows)
        fro = fl_acc[b].reshape(block_rows, vocab_rows)
        prob = jnp.exp(pol - cols[span, 1:2])
        value = cols[span, 4:5] * (
            cols[span, 3:4] * (chosen_of(span).astype(f32) - prob)
            + kl_weight * prob * ((pol - fro) - cols[span, 2:3])
        )
        grad[pl.ds(b * 4, 4)] = value.astype(bf16).reshape(4, 2, 16, vocab_rows)

    def product(core, q):
        left = grad[:, core].reshape(tokens // 2, vocab_rows)
        right = pw[:, q * quarter : (q + 1) * quarter]
        made = jnp.dot(left, right, preferred_element_type=f32)
        return made.reshape(4, 2, 2, 16, quarter)

    def sib_copy(q):
        return put(sib_out.at[q], sib_in.at[q], sib_send.at[q], sib_recv.at[q], sibling)

    def for_sibling(q):
        sib_out[q] = product(1 - c, q).astype(bf16)
        sib_copy(q).start()

    flip_x, flip_y = dev(z, y, 1 - x, c), dev(z, 1 - y, x, c)

    def sides(q):
        order = SCATTER[q]
        own, other = (y, x) if order[0] == "y" else (x, y)
        to_first, to_other = (flip_y, flip_x) if order[0] == "y" else (flip_x, flip_y)
        return own, other, to_first, to_other

    def s1_copy(q, zz):
        _, _, to_first, _ = sides(q)
        return put(s1.at[q, zz], r1.at[q, zz], s1_send.at[q, zz], s1_recv.at[q, zz], to_first)

    def s2_copy(q, zz):
        _, _, _, to_other = sides(q)
        return put(s2.at[q, zz], r2.at[q, zz], s2_send.at[q, zz], s2_recv.at[q, zz], to_other)

    def z_slot(ref, q, way, dest):
        return ref.at[q, way, dest]

    def z_copy(q, way, dest):
        where = dev(z + 1, y, x, c) if way == 0 else dev(z - 1, y, x, c)
        return put(
            z_slot(zs, q, way, dest), z_slot(zr, q, way, dest),
            z_send.at[q, way, dest], z_recv.at[q, way, dest], where,
        )

    def for_own(q):
        made = product(c, q)
        sib_copy(q).wait_recv()
        made = made + sib_in[q].astype(f32)
        own, other, _, _ = sides(q)
        for i in range(2):
            for j in range(2):
                acc[q, :, i, j] = made[:, i, j] if SCATTER[q][0] == "y" else made[:, j, i]
        for zz in range(4):
            s1[q, zz] = acc[q, zz, 1 - own].astype(bf16)
            s1_copy(q, zz).start()

    for_sibling(2)
    for_sibling(3)
    for_own(2)
    for_sibling(0)
    for_own(3)
    for_sibling(1)
    for_own(0)
    for_own(1)

    def take_first(q, zz):
        own, other, _, _ = sides(q)
        s1_copy(q, zz).wait_recv()
        acc[q, zz, own] += r1[q, zz].astype(f32)
        if SCATTER[q][2] == "z":
            s2[q, zz] = acc[q, zz, own, 1 - other].astype(bf16)
            s2_copy(q, zz).start()

    def line_value(q, dest):
        own, _, _, _ = sides(q)
        return acc.at[q, dest, own]

    def line_step(q, k):
        @pl.when(z + k <= 3)
        def _():
            dest = z + k
            held = line_value(q, dest)

            @pl.when(z > 0)
            def _():
                z_copy(q, 0, dest).wait_recv()
                held[...] += z_slot(zr, q, 0, dest)[...].astype(f32)

            z_slot(zs, q, 0, dest)[...] = held[...].astype(bf16)
            z_copy(q, 0, dest).start()

        @pl.when(z - k >= 0)
        def _():
            dest = z - k
            held = line_value(q, dest)

            @pl.when(z < 3)
            def _():
                z_copy(q, 1, dest).wait_recv()
                held[...] += z_slot(zr, q, 1, dest)[...].astype(f32)

            z_slot(zs, q, 1, dest)[...] = held[...].astype(bf16)
            z_copy(q, 1, dest).start()

    def line_end(q):
        held = line_value(q, z)

        @pl.when(z > 0)
        def _():
            z_copy(q, 0, z).wait_recv()
            held[...] += z_slot(zr, q, 0, z)[...].astype(f32)

        @pl.when(z < 3)
        def _():
            z_copy(q, 1, z).wait_recv()
            held[...] += z_slot(zr, q, 1, z)[...].astype(f32)

    def direct_copy(q, dest, slot):
        return put(
            zs.at[q, 0, dest, 0], zr.at[q, 0, slot, 0],
            z_send.at[q, 0, dest], z_recv.at[q, 0, slot], dev(dest, y, x, c),
        )

    for zz in range(4):
        for q in (2, 3):
            take_first(q, zz)
    for k in (3, 2, 1):
        for q in (2, 3):
            line_step(q, k)
        for q in (0, 1):
            take_first(q, 3 - k)
    for q in (0, 1):
        take_first(q, 3)
    for q in (2, 3):
        line_end(q)
        own, other, _, _ = sides(q)
        s2[q, 0] = acc[q, z, own, 1 - other].astype(bf16)
        s2_copy(q, 0).start()
    for zz in range(4):
        for q in (0, 1):
            own, other, _, _ = sides(q)
            s2_copy(q, zz).wait_recv()
            acc[q, zz, own, other] += r2[q, zz].astype(f32)

            @pl.when(z != zz)
            def _():
                zs[q, 0, zz, 0] = acc[q, zz, own, other].astype(bf16)
                direct_copy(q, zz, z).start()

    for q in (2, 3):
        own, other, _, _ = sides(q)
        s2_copy(q, 0).wait_recv()
        done = acc[q, z, own, other] + r2[q, 0].astype(f32)
        out[:, q * quarter : (q + 1) * quarter] = done.astype(bf16)
    for q in (0, 1):
        own, other, _, _ = sides(q)
        done = acc[q, z, own, other]
        for k in range(1, 4):
            source = (z + k) % 4
            direct_copy(q, source, source).wait_recv()
            done = done + zr[q, 0, source, 0].astype(f32)
        out[:, q * quarter : (q + 1) * quarter] = done.astype(bf16)

    for k in range(1, 8):
        st1_copy(k, plane).wait_send()
    for k in range(1, 4):
        st2_copy(k, z).wait_send()
    for q in range(4):
        sib_copy(q).wait_send()
        for zz in range(4):
            s1_copy(q, zz).wait_send()
        for zz in range(4 if SCATTER[q][2] == "z" else 1):
            s2_copy(q, zz).wait_send()
        if SCATTER[q][2] == "z":
            for k in range(1, 4):
                direct_copy(q, (z + k) % 4, z).wait_send()
            continue
        for k in (3, 2, 1):
            @pl.when(z + k <= 3)
            def _():
                z_copy(q, 0, z + k).wait_send()

            @pl.when(z - k >= 0)
            def _():
                z_copy(q, 1, z - k).wait_send()


def fused(ph, fh, pw, fw, actions, behavior, sign, size, mask):
    own_rows, width = ph.shape
    vocab_rows = pw.shape[0]
    tokens = actions.shape[0]
    quarter = width // 4
    vmem, dma = pltpu.VMEM, pltpu.SemaphoreType.DMA
    row = lambda a: a.reshape(1, tokens)
    in_vmem = pl.BlockSpec(memory_space=pltpu.VMEM)
    in_hbm = pl.BlockSpec(memory_space=pl.ANY)
    out, loss = pl.pallas_call(
        kernel,
        out_shape=(
            jax.ShapeDtypeStruct((own_rows, width), bf16),
            jax.ShapeDtypeStruct((1, 1), f32),
        ),
        in_specs=[in_vmem, in_vmem, in_hbm, in_hbm] + [in_vmem] * 5,
        out_specs=(in_vmem, in_vmem),
        scratch_shapes=[
            vmem((2, 4, 2, 2, 2, own_rows, width), bf16),
            vmem((vocab_rows, width), bf16),
            vmem((vocab_rows, width), bf16),
            vmem((4, 2, 2, 2, own_rows, vocab_rows), f32),
            vmem((4, 2, 2, 2, own_rows, vocab_rows), f32),
            vmem((tokens, 128), f32),
            vmem((128, tokens), f32),
            vmem((16, 2, own_rows, vocab_rows), bf16),
            vmem((8, 8, tokens), f32),
            vmem((4, 8, tokens), f32),
            vmem((4, 4, 2, 2, own_rows, quarter), bf16),
            vmem((4, 4, 2, 2, own_rows, quarter), bf16),
            vmem((4, 4, 2, 2, own_rows, quarter), f32),
            vmem((4, 4, 2, own_rows, quarter), bf16),
            vmem((4, 4, 2, own_rows, quarter), bf16),
            vmem((4, 4, own_rows, quarter), bf16),
            vmem((4, 4, own_rows, quarter), bf16),
            vmem((4, 2, 4, 2, own_rows, quarter), bf16),
            vmem((4, 2, 4, 2, own_rows, quarter), bf16),
            dma((2,)), dma((4, 16, 5)), dma((4, 16)), dma((4, 16)),
            dma((8,)), dma((8,)), dma((4,)), dma((4,)),
            dma((4,)), dma((4,)), dma((4, 4)), dma((4, 4)),
            dma((4, 4)), dma((4, 4)), dma((4, 2, 4)), dma((4, 2, 4)),
        ],
        compiler_params=pltpu.CompilerParams(
            collective_id=0, has_side_effects=True, vmem_limit_bytes=60 * 1024 * 1024
        ),
        cost_estimate=pl.CostEstimate(
            flops=6 * tokens * width * vocab_rows,
            bytes_accessed=4 * width * vocab_rows,
            transcendentals=3 * tokens * vocab_rows,
        ),
        name="fused",
    )(ph, fh, pw, fw, row(actions), row(behavior), row(sign), row(size), row(mask))
    return out, loss.reshape(1)


def solution(mesh):
    placed = (
        P(("groups", "vocab"), None),
        P(("groups", "vocab"), None),
        P("vocab", None),
        P("vocab", None),
        P("groups"),
        P("groups"),
        P("groups"),
        P("groups"),
        P("groups"),
    )
    body = fused if dict(mesh.shape) == {"groups": 1, "vocab": 32} else shards
    return jax.shard_map(
        body,
        mesh=mesh,
        in_specs=placed,
        out_specs=(P(("groups", "vocab"), None), P("groups")),
        check_vma=False,
    )
```
